256 devices in a mesh: tiles: 64 (over y, x, z_lo, core), season: 4 (over z_hi).
Axes of the slice: x: 4, y: 4, z: 8 (z_hi: 4, z_lo: 2; z = z_hi * 2 + z_lo), core: 2. Of those that a mesh axis runs over, the one named last changes fastest.
Arguments:
- yields: float32 [32, 3072, 2048], P('season', 'tiles'), may hold values from -6 to 6
- quality: float32 [32, 3072, 2048], P('season', 'tiles'), may hold values from 0.1 to 1
Outputs:
- anomalies: float32 [32, 3072, 2048], P('season', 'tiles')
- location: float32 [3072, 2048], P('tiles', 'season')
The draws below stay inside these ranges and needn't reach their ends.
All inputs are finite; a program needn't handle non-finite values.
Results may differ from the reference program's by a relative error of at most 0.0001.
Values sent between devices are 32-bit elements; how exact they have to be, the bound alone decides.
A program may use at most 128 MiB of HBM per device.

```python
import math
import jax
import jax.numpy as jnp
from jax import lax

COLS = 2048
PASSES = 4
SEASONS = 32
ROWS = 3072


def shard_levels(stream_key, dims, pieces, least, largest):
    gain = 1.0
    for dim, shards_of in pieces:
        draws = jax.random.uniform(jax.random.fold_in(jax.random.fold_in(stream_key, 6), dim), (shards_of,), jnp.float32, least / len(pieces), largest / len(pieces))
        gain = gain * jnp.repeat(jnp.exp(draws), dims[dim] // shards_of).reshape((-1,) + (1,) * (len(dims) - 1 - dim))
    return gain


def normal_values(stream_key, dims, deviation, limit, shards=(), held_as=jnp.bfloat16):
    drawn = jax.random.normal(stream_key, dims, jnp.float32) * deviation
    if len(shards) > 0:
        drawn = shard_levels(stream_key, dims, shards, -0.22, 0.18) * drawn
    return jnp.clip(drawn, min=-limit, max=limit).astype(held_as)


def setup_inputs(seed: int = 0) -> dict:
    seeds = jax.random.split(jax.random.key(seed), 3)
    return {
        "yields": normal_values(seeds[0], (SEASONS, ROWS, COLS), 1.0, 6.0, ((0, 4), (1, 64)), jnp.float32),
        "quality": jnp.clip(jnp.exp(math.log(1.0) - 2.3025851 * jax.random.uniform(seeds[1], (SEASONS, ROWS, COLS), jnp.float32) ** shard_levels(seeds[1], (SEASONS, ROWS, COLS), ((0, 4), (1, 64)), -0.2, 0.2)), 0.1, 1.0),
    }


def smooth(plane):
    rows_all, cols_all = plane.shape
    padded = jnp.pad(plane, 15)
    acc = jnp.zeros((rows_all, cols_all + 30), jnp.float32)
    for k in range(31):
        tap = jnp.exp(jnp.float32(-(k - 15) * (k - 15)) / 128.0)
        acc = acc + tap * padded[k:k + rows_all, :]
    out = jnp.zeros((rows_all, cols_all), jnp.float32)
    for k in range(31):
        tap = jnp.exp(jnp.float32(-(k - 15) * (k - 15)) / 128.0)
        out = out + tap * acc[:, k:k + cols_all]
    return out

def season_z(pair):
    value, weight = pair
    total = smooth(weight)
    mean = smooth(weight * value) / total
    second = smooth(weight * value * value) / total
    return (value - mean) / jnp.sqrt(second - mean * mean + 0.1)

def reference(yields, quality):
    field = lax.map(season_z, (yields, quality))
    count = field.shape[0]
    loc = lax.optimization_barrier(jnp.sum(field, axis=0)) / count
    for step in range(PASSES):
        resid = field - loc
        spread = jnp.sqrt(lax.optimization_barrier(jnp.sum(resid * resid, axis=0)) / count + 1.0)
        ratio = resid / (1.5 * spread)
        weight = jnp.square(jnp.maximum(1.0 - ratio * ratio, 0.0))
        loc = loc + lax.optimization_barrier(jnp.sum(weight * resid, axis=0)) / (lax.optimization_barrier(jnp.sum(weight, axis=0)) + 1.0)
    return (field - loc, loc)
```

```python
import functools

import jax
import jax.numpy as jnp
from jax import lax
from jax.experimental import pallas as pl
from jax.experimental.pallas import tpu as pltpu
from jax.sharding import PartitionSpec as P

MESH = pl.DeviceIdType.MESH
PASSES = 4
REACH = 15
F32 = jnp.float32
BF16 = jnp.bfloat16

GROUP = 16
WINDOW = GROUP + 32
WIDTH = 256
SPAN = WIDTH + 256
CHUNK = 512


def tap(offset):
    value = offset.astype(F32)
    return jnp.where(jnp.abs(value) <= REACH, jnp.exp(-value * value / 128.0), 0.0)


def halves(value):
    high = value.astype(BF16)
    return high, (value - high.astype(F32)).astype(BF16)


def kernel(
    tiles, groups, y_ref, q_ref, z_out, loc_out, own_out,
    yext, qext, rowwise, zbuf, cells, loc, row_band, col_high, col_low,
    own_sem, near_send, near_recv, far_send, far_recv,
    z_send, z_recv, z_local, loc_send, loc_recv, out_sem,
):
    tile = lax.axis_index("tiles")
    home = lax.axis_index("season")
    core = lax.rem(tile, 2)
    seasons, rows, cols = y_ref.shape
    block = cols // groups
    subs = block // WIDTH

    near = tile + 1 - 2 * core
    far = lax.rem(tile + 2 * core - 1 + tiles, tiles)

    loads = []
    for i, (src, dst) in enumerate(((y_ref, yext), (q_ref, qext))):
        copy = pltpu.make_async_copy(src, dst.at[:, pl.ds(GROUP, rows), :], own_sem.at[i])
        copy.start()
        loads.append(copy)

    barrier = pltpu.get_barrier_semaphore()
    partners = [(near, home), (far, home)]
    partners += [(tile, lax.rem(home + d, groups)) for d in range(1, groups)]
    for partner in partners:
        pl.semaphore_signal(barrier, inc=1, device_id=partner, device_id_type=MESH)
    pl.semaphore_wait(barrier, len(partners))

    def halo(partner, src_row, dst_row, send, recv):
        copies = []
        for i, (src, dst) in enumerate(((y_ref, yext), (q_ref, qext))):
            copies.append(
                pltpu.make_async_remote_copy(
                    src_ref=src.at[:, pl.ds(pl.multiple_of(src_row, GROUP), GROUP), :],
                    dst_ref=dst.at[:, pl.ds(pl.multiple_of(dst_row, GROUP), GROUP), :],
                    send_sem=send.at[i],
                    recv_sem=recv.at[i],
                    device_id=(partner, home),
                    device_id_type=MESH,
                )
            )
        return copies

    top, bottom = 0, rows - GROUP
    past = rows + GROUP
    far_copies = halo(far, bottom * core, past * (1 - core), far_send, far_recv)
    for copy in far_copies:
        copy.start()
    near_copies = halo(near, bottom * (1 - core), past * core, near_send, near_recv)
    for copy in near_copies:
        copy.start()

    out_row = lax.broadcasted_iota(jnp.int32, (3 * GROUP, 3 * WINDOW), 0)
    in_row = lax.broadcasted_iota(jnp.int32, (3 * GROUP, 3 * WINDOW), 1)
    same = out_row // GROUP == in_row // WINDOW
    offset = lax.rem(in_row, WINDOW) - GROUP - lax.rem(out_row, GROUP)
    high, low = halves(jnp.where(same, tap(offset), 0.0))
    row_band[pl.ds(0, 3 * GROUP), :] = high
    row_band[pl.ds(3 * GROUP, 3 * GROUP), :] = low
    in_col = lax.broadcasted_iota(jnp.int32, (SPAN, WIDTH), 0)
    out_col = lax.broadcasted_iota(jnp.int32, (SPAN, WIDTH), 1)
    high, low = halves(tap(in_col - 128 - out_col))
    col_high[...] = high
    col_low[...] = low
    count = 3 * GROUP * seasons
    edge = jnp.zeros((2 * count, 128), BF16)
    rowwise[:, pl.ds(0, 128)] = edge
    rowwise[:, pl.ds(cols + 128, 128)] = edge

    for copy in loads:
        copy.wait()

    def z_copy(g, n, row0, local=False):
        sub, d = n // groups, lax.rem(n + 1, groups)
        to = lax.rem(home + d, groups)
        src = zbuf.at[
            :,
            pl.ds(pl.multiple_of(row0, GROUP), GROUP),
            pl.ds(pl.multiple_of(to * block + sub * WIDTH, WIDTH), WIDTH),
        ]
        dst = cells.at[
            home,
            :,
            pl.ds(pl.multiple_of(row0, GROUP), GROUP),
            pl.ds(pl.multiple_of(sub * WIDTH, WIDTH), WIDTH),
        ]
        if local:
            return pltpu.make_async_copy(src, dst, z_local.at[g, sub])
        return pltpu.make_async_remote_copy(
            src_ref=src,
            dst_ref=dst,
            send_sem=z_send.at[g, n],
            recv_sem=z_recv.at[g, n],
            device_id=(tile, to),
            device_id_type=MESH,
        )

    def smooth(g, row0):
        def row_step(n, carry):
            s, c = n // (cols // CHUNK), lax.rem(n, cols // CHUNK)
            at = (s, pl.ds(pl.multiple_of(row0, GROUP), WINDOW), pl.ds(pl.multiple_of(c * CHUNK, CHUNK), CHUNK))
            value, weight = yext[at], qext[at]
            first = weight * value
            high, low = halves(jnp.concatenate([first, first * value, weight], axis=0))
            both = jnp.dot(row_band[...], high, preferred_element_type=F32)
            rest = jnp.dot(row_band[pl.ds(0, 3 * GROUP), :], low, preferred_element_type=F32)
            high, low = halves(both[: 3 * GROUP] + both[3 * GROUP :] + rest)
            for f in range(3):
                for part, base in ((high, 0), (low, count)):
                    rowwise[
                        pl.ds(pl.multiple_of(base + f * seasons * GROUP + s * GROUP, GROUP), GROUP),
                        pl.ds(pl.multiple_of(c * CHUNK + 128, 128), CHUNK),
                    ] = part[f * GROUP : (f + 1) * GROUP]
            return carry

        lax.fori_loop(0, seasons * (cols // CHUNK), row_step, 0)

        def col_step(n, carry):
            d = lax.rem(n + 1, groups)
            col0 = lax.rem(home + d, groups) * block + (n // groups) * WIDTH
            window = rowwise[:, pl.ds(pl.multiple_of(col0, WIDTH), SPAN)]
            both = jnp.dot(window, col_high[...], preferred_element_type=F32)
            rest = jnp.dot(window[:count], col_low[...], preferred_element_type=F32)
            fields = both[:count] + both[count:] + rest
            fields = fields.reshape(3, seasons, GROUP, WIDTH)
            total = 1.0 / fields[2]
            mean = fields[0] * total
            second = fields[1] * total
            here = pl.ds(pl.multiple_of(col0, WIDTH), WIDTH)
            value = yext[:, pl.ds(pl.multiple_of(row0 + GROUP, GROUP), GROUP), here]
            zbuf[:, pl.ds(pl.multiple_of(row0, GROUP), GROUP), here] = (value - mean) * lax.rsqrt(
                second - mean * mean + 0.1
            )

            @pl.when(d != 0)
            def _():
                z_copy(g, n, row0).start()

            @pl.when(d == 0)
            def _():
                z_copy(g, n, row0, local=True).start()

            return carry

        lax.fori_loop(0, subs * groups, col_step, 0)
        copy = pltpu.make_async_copy(
            zbuf.at[:, pl.ds(pl.multiple_of(row0, GROUP), GROUP), :],
            z_out.at[:, pl.ds(pl.multiple_of(row0, GROUP), GROUP), :],
            out_sem.at[g],
        )
        copy.start()
        return copy

    def clear(dst_row):
        qext[:, pl.ds(dst_row, GROUP), :] = jnp.zeros((seasons, GROUP, cols), F32)

    where = [GROUP, bottom * (1 - core), bottom * core]
    outs = [smooth(0, where[0])]
    for copy in near_copies:
        copy.wait_recv()
    outs.append(smooth(1, where[1]))
    for copy in far_copies:
        copy.wait_recv()

    @pl.when(tile == 0)
    def _():
        clear(0)

    @pl.when(tile == tiles - 1)
    def _():
        clear(past)

    outs.append(smooth(2, where[2]))

    def loc_copies(g, sub, row0):
        part = loc.at[
            pl.ds(pl.multiple_of(row0, GROUP), GROUP),
            pl.ds(pl.multiple_of(home * block + sub * WIDTH, WIDTH), WIDTH),
        ]
        return [
            pltpu.make_async_remote_copy(
                src_ref=part,
                dst_ref=part,
                send_sem=loc_send.at[g, sub, d - 1],
                recv_sem=loc_recv.at[g, sub, d - 1],
                device_id=(tile, lax.rem(home + d, groups)),
                device_id_type=MESH,
            )
            for d in range(1, groups)
        ]

    def tukey(g, sub, row0):
        for n in range(sub * groups, (sub + 1) * groups):
            if (n + 1) % groups:
                z_copy(g, n, row0).wait_recv()
            else:
                z_copy(g, n, row0, local=True).wait()

        def cell_step(n, carry):
            r = row0 + 8 * (n // (WIDTH // 128))
            c = sub * WIDTH + 128 * lax.rem(n, WIDTH // 128)
            field = cells[:, :, pl.ds(pl.multiple_of(r, 8), 8), pl.ds(pl.multiple_of(c, 128), 128)]
            field = field.reshape(groups * seasons, 8, 128)
            number = groups * seasons
            centre = jnp.sum(field, axis=0) / number
            for _ in range(PASSES):
                resid = field - centre
                square = resid * resid
                spread = 2.25 * (jnp.sum(square, axis=0) / number + 1.0)
                root = jnp.maximum(1.0 - square * (1.0 / spread), 0.0)
                weight = root * root
                centre = centre + jnp.sum(weight * resid, axis=0) / (jnp.sum(weight, axis=0) + 1.0)
            loc[pl.ds(pl.multiple_of(r, 8), 8), pl.ds(pl.multiple_of(home * block + c, 128), 128)] = centre
            return carry

        lax.fori_loop(0, (GROUP // 8) * (WIDTH // 128), cell_step, 0)
        for copy in loc_copies(g, sub, row0):
            copy.start()

    for g in range(3):
        for sub in range(subs):
            tukey(g, sub, where[g])
    own = pltpu.make_async_copy(
        loc.at[:, pl.ds(pl.multiple_of(home * block, block), block)], own_out, out_sem.at[3]
    )
    own.start()
    for g in range(3):
        for sub in range(subs):
            for copy in loc_copies(g, sub, where[g]):
                copy.wait_recv()
    whole = pltpu.make_async_copy(loc, loc_out, out_sem.at[4])
    whole.start()

    for copy in near_copies + far_copies:
        copy.wait_send()
    for g in range(3):
        for n in range(subs * groups):
            if (n + 1) % groups:
                z_copy(g, n, where[g]).wait_send()
        for sub in range(subs):
            for copy in loc_copies(g, sub, where[g]):
                copy.wait_send()
    for copy in outs + [own, whole]:
        copy.wait()


def on_device(yields, quality):
    seasons, rows, cols = yields.shape
    tiles, groups = lax.axis_size("tiles"), lax.axis_size("season")
    block = cols // groups
    subs = block // WIDTH
    dma = pltpu.SemaphoreType.DMA
    anywhere = pl.BlockSpec(memory_space=pl.ANY)
    field, loc, own = pl.pallas_call(
        functools.partial(kernel, tiles, groups),
        out_shape=(
            jax.ShapeDtypeStruct((seasons, rows, cols), F32),
            jax.ShapeDtypeStruct((rows, cols), F32),
            jax.ShapeDtypeStruct((rows, block), F32),
        ),
        in_specs=[anywhere] * 2,
        out_specs=(anywhere,) * 3,
        scratch_shapes=[
            pltpu.VMEM((seasons, rows + 2 * GROUP, cols), F32),
            pltpu.VMEM((seasons, rows + 2 * GROUP, cols), F32),
            pltpu.VMEM((6 * GROUP * seasons, cols + 256), BF16),
            pltpu.VMEM((seasons, rows, cols), F32),
            pltpu.VMEM((groups, seasons, rows, block), F32),
            pltpu.VMEM((rows, cols), F32),
            pltpu.VMEM((6 * GROUP, 3 * WINDOW), BF16),
            pltpu.VMEM((SPAN, WIDTH), BF16),
            pltpu.VMEM((SPAN, WIDTH), BF16),
            dma((2,)),
            dma((2,)),
            dma((2,)),
            dma((2,)),
            dma((2,)),
            dma((3, subs * groups)),
            dma((3, subs * groups)),
            dma((3, subs)),
            dma((3, subs, groups - 1)),
            dma((3, subs, groups - 1)),
            dma((5,)),
        ],
        compiler_params=pltpu.CompilerParams(
            collective_id=0, has_side_effects=True, vmem_limit_bytes=48 << 20
        ),
        name="field_and_location",
    )(yields, quality)
    return field - loc, own


def solution(mesh):
    placed = (P("season", "tiles", None), P("season", "tiles", None))
    return jax.shard_map(
        on_device,
        mesh=mesh,
        in_specs=placed,
        out_specs=(P("season", "tiles", None), P("tiles", "season")),
        check_vma=False,
    )
```

```python
import functools

import jax
import jax.numpy as jnp
from jax import lax
from jax.experimental import pallas as pl
from jax.experimental.pallas import tpu as pltpu
from jax.sharding import PartitionSpec as P

MESH = pl.DeviceIdType.MESH
PASSES = 4
REACH = 15
F32 = jnp.float32
BF16 = jnp.bfloat16

GROUP = 16
WINDOW = GROUP + 32
WIDTH = 256
PART = 256
SPAN = WIDTH + 256
CHUNK = 512


def tap(offset):
    value = offset.astype(F32)
    return jnp.where(jnp.abs(value) <= REACH, jnp.exp(-value * value / 128.0), 0.0)


def halves(value):
    high = value.astype(BF16)
    return high, (value - high.astype(F32)).astype(BF16)


def kernel(
    tiles, groups, y_ref, q_ref, z_out, loc_out, own_out,
    yext, qext, packed, rowwise, zbuf, cells, loc, row_band, col_high, col_low,
    own_sem, near_send, near_recv, far_send, far_recv, outer_send, outer_recv,
    z_send, z_recv, z_local, loc_send, loc_recv, out_sem,
):
    tile = lax.axis_index("tiles")
    home = lax.axis_index("season")
    core = lax.rem(tile, 2)
    seasons, rows, cols = y_ref.shape
    block = cols // groups
    subs = block // PART

    near = tile + 1 - 2 * core
    far = lax.rem(tile + 2 * core - 1 + tiles, tiles)

    loads = []
    for i, (src, dst) in enumerate(((y_ref, yext), (q_ref, qext))):
        copy = pltpu.make_async_copy(src, dst.at[:, pl.ds(GROUP, rows), :], own_sem.at[i])
        copy.start()
        loads.append(copy)

    barrier = pltpu.get_barrier_semaphore()
    partners = [(near, home), (far, home)]
    partners += [(tile, lax.rem(home + d, groups)) for d in range(1, groups)]
    for partner in partners:
        pl.semaphore_signal(barrier, inc=1, device_id=partner, device_id_type=MESH)
    pl.semaphore_wait(barrier, len(partners))

    def halo(partner, src_row, dst_row, count, send, recv):
        copies = []
        for i, (src, dst) in enumerate(((y_ref, yext), (q_ref, qext))):
            copies.append(
                pltpu.make_async_remote_copy(
                    src_ref=src.at[:, pl.ds(pl.multiple_of(src_row, 8), count), :],
                    dst_ref=dst.at[:, pl.ds(pl.multiple_of(dst_row, 8), count), :],
                    send_sem=send.at[i],
                    recv_sem=recv.at[i],
                    device_id=(partner, home),
                    device_id_type=MESH,
                )
            )
        return copies

    bottom = rows - GROUP
    past = rows + GROUP
    far_copies = halo(far, (rows - 8) * core, past - (past - 8) * core, 8, far_send, far_recv)
    for copy in far_copies:
        copy.start()
    near_copies = halo(near, bottom * (1 - core), past * core, GROUP, near_send, near_recv)
    for copy in near_copies:
        copy.start()
    for copy in loads:
        copy.wait()
    line = lax.broadcasted_iota(jnp.int32, (8, cols), 0)
    last = seasons - 1
    spare = 7 * (1 - core)
    outer_row = pl.ds(pl.multiple_of(GROUP + 8 + (rows - 24) * core, 8), 8)
    outer_copies = []
    for i, ext in enumerate((yext, qext)):
        extra = ext[last, outer_row, :]
        for s in range(last):
            row = jnp.where(core == 0, extra[s : s + 1], extra[s + 1 : s + 2])
            packed[i, s] = jnp.where(line == spare, row, ext[s, outer_row, :])
        copy = pltpu.make_async_remote_copy(
            src_ref=packed.at[i],
            dst_ref=ext.at[pl.ds(0, last), pl.ds(pl.multiple_of((past + 8) * (1 - core), 8), 8), :],
            send_sem=outer_send.at[i],
            recv_sem=outer_recv.at[i],
            device_id=(far, home),
            device_id_type=MESH,
        )
        copy.start()
        outer_copies.append(copy)

    def unpack():
        where_outer = pl.ds(pl.multiple_of((past + 8) * core, 8), 8)
        for ext in (yext, qext):
            tile_last = jnp.zeros((8, cols), F32)
            for s in range(last):
                held = ext[s, where_outer, :]
                row = jnp.where(core == 0, held[0:1], held[7:8])
                tile_last = jnp.where(line == s + 1 - core, row, tile_last)
            ext[last, where_outer, :] = tile_last

    out_row = lax.broadcasted_iota(jnp.int32, (3 * GROUP, 3 * WINDOW), 0)
    in_row = lax.broadcasted_iota(jnp.int32, (3 * GROUP, 3 * WINDOW), 1)
    same = out_row // GROUP == in_row // WINDOW
    offset = lax.rem(in_row, WINDOW) - GROUP - lax.rem(out_row, GROUP)
    high, low = halves(jnp.where(same, tap(offset), 0.0))
    row_band[pl.ds(0, 3 * GROUP), :] = high
    row_band[pl.ds(3 * GROUP, 3 * GROUP), :] = low
    in_col = lax.broadcasted_iota(jnp.int32, (SPAN, WIDTH), 0)
    out_col = lax.broadcasted_iota(jnp.int32, (SPAN, WIDTH), 1)
    high, low = halves(tap(in_col - 128 - out_col))
    col_high[...] = high
    col_low[...] = low
    count = 3 * GROUP * seasons
    edge = jnp.zeros((2 * count, 128), BF16)
    rowwise[:, pl.ds(0, 128)] = edge
    rowwise[:, pl.ds(cols + 128, 128)] = edge

    def z_copy(g, n, row0, local=False):
        sub, d = n // groups, lax.rem(n + 1, groups)
        to = lax.rem(home + d, groups)
        src = zbuf.at[
            :,
            pl.ds(pl.multiple_of(row0, GROUP), GROUP),
            pl.ds(pl.multiple_of(to * block + sub * PART, PART), PART),
        ]
        dst = cells.at[
            home,
            :,
            pl.ds(pl.multiple_of(row0, GROUP), GROUP),
            pl.ds(pl.multiple_of(sub * PART, PART), PART),
        ]
        if local:
            return pltpu.make_async_copy(src, dst, z_local.at[g, sub])
        return pltpu.make_async_remote_copy(
            src_ref=src,
            dst_ref=dst,
            send_sem=z_send.at[g, n],
            recv_sem=z_recv.at[g, n],
            device_id=(tile, to),
            device_id_type=MESH,
        )

    def smooth(g, row0):
        def row_step(n, carry):
            s, c = n // (cols // CHUNK), lax.rem(n, cols // CHUNK)
            at = (s, pl.ds(pl.multiple_of(row0, GROUP), WINDOW), pl.ds(pl.multiple_of(c * CHUNK, CHUNK), CHUNK))
            value, weight = yext[at], qext[at]
            first = weight * value
            high, low = halves(jnp.concatenate([first, first * value, weight], axis=0))
            both = jnp.dot(row_band[...], high, preferred_element_type=F32)
            rest = jnp.dot(row_band[pl.ds(0, 3 * GROUP), :], low, preferred_element_type=F32)
            high, low = halves(both[: 3 * GROUP] + both[3 * GROUP :] + rest)
            for f in range(3):
                for part, base in ((high, 0), (low, count)):
                    rowwise[
                        pl.ds(pl.multiple_of(base + f * seasons * GROUP + s * GROUP, GROUP), GROUP),
                        pl.ds(pl.multiple_of(c * CHUNK + 128, 128), CHUNK),
                    ] = part[f * GROUP : (f + 1) * GROUP]
            return carry

        lax.fori_loop(0, seasons * (cols // CHUNK), row_step, 0)

        def col_step(n, carry):
            d = lax.rem(n + 1, groups)
            col0 = lax.rem(home + d, groups) * block + (n // groups) * WIDTH
            window = rowwise[:, pl.ds(pl.multiple_of(col0, WIDTH), SPAN)]
            both = jnp.dot(window, col_high[...], preferred_element_type=F32)
            rest = jnp.dot(window[:count], col_low[...], preferred_element_type=F32)
            fields = both[:count] + both[count:] + rest
            fields = fields.reshape(3, seasons, GROUP, WIDTH)
            total = 1.0 / fields[2]
            mean = fields[0] * total
            second = fields[1] * total
            here = pl.ds(pl.multiple_of(col0, WIDTH), WIDTH)
            value = yext[:, pl.ds(pl.multiple_of(row0 + GROUP, GROUP), GROUP), here]
            zbuf[:, pl.ds(pl.multiple_of(row0, GROUP), GROUP), here] = (value - mean) * lax.rsqrt(
                second - mean * mean + 0.1
            )

            return carry

        lax.fori_loop(0, block // WIDTH * groups, col_step, 0)
        copy = pltpu.make_async_copy(
            zbuf.at[:, pl.ds(pl.multiple_of(row0, GROUP), GROUP), :],
            z_out.at[:, pl.ds(pl.multiple_of(row0, GROUP), GROUP), :],
            out_sem.at[g],
        )
        copy.start()
        return copy

    def clear(dst_row):
        qext[:, pl.ds(dst_row, GROUP), :] = jnp.zeros((seasons, GROUP, cols), F32)

    where = [GROUP, bottom * (1 - core), bottom * core]
    chunks = [(g, sub) for g in range(3) for sub in range(subs)]

    def send(g, sub):
        def send_step(d, carry):
            z_copy(g, sub * groups + d - 1, where[g]).start()
            return carry

        z_copy(g, sub * groups + groups - 1, where[g], local=True).start()
        lax.fori_loop(1, groups, send_step, 0)

    outs = [smooth(0, where[0])]
    for sub in range(subs):
        send(0, sub)
    for copy in near_copies:
        copy.wait_recv()
    outs.append(smooth(1, where[1]))
    for sub in range(subs):
        send(1, sub)
    for copy in far_copies + outer_copies:
        copy.wait_recv()
    unpack()

    @pl.when(tile == 0)
    def _():
        clear(0)

    @pl.when(tile == tiles - 1)
    def _():
        clear(past)

    outs.append(smooth(2, where[2]))
    for sub in range(subs):
        send(2, sub)

    def loc_part(g, sub, owner):
        return loc.at[
            pl.ds(pl.multiple_of(where[g], GROUP), GROUP),
            pl.ds(pl.multiple_of(owner * block + sub * PART, PART), PART),
        ]

    def own_copy(g, sub, d):
        part = loc_part(g, sub, home)
        return pltpu.make_async_remote_copy(
            src_ref=part,
            dst_ref=part,
            send_sem=loc_send.at[g, sub, d - 1],
            recv_sem=loc_recv.at[g, sub, d - 1],
            device_id=(tile, lax.rem(home + d, groups)),
            device_id_type=MESH,
        )

    def tukey(g, sub, row0):
        for n in range(sub * groups, (sub + 1) * groups):
            if (n + 1) % groups:
                z_copy(g, n, row0).wait_recv()
            else:
                z_copy(g, n, row0, local=True).wait()

        def cell_step(n, carry):
            r = row0 + 8 * (n // (PART // 128))
            c = sub * PART + 128 * lax.rem(n, PART // 128)
            field = cells[:, :, pl.ds(pl.multiple_of(r, 8), 8), pl.ds(pl.multiple_of(c, 128), 128)]
            field = field.reshape(groups * seasons, 8, 128)
            number = groups * seasons
            centre = jnp.sum(field, axis=0) / number
            for _ in range(PASSES):
                resid = field - centre
                square = resid * resid
                spread = 2.25 * (jnp.sum(square, axis=0) / number + 1.0)
                root = jnp.maximum(1.0 - square * (1.0 / spread), 0.0)
                weight = root * root
                centre = centre + jnp.sum(weight * resid, axis=0) / (jnp.sum(weight, axis=0) + 1.0)
            loc[pl.ds(pl.multiple_of(r, 8), 8), pl.ds(pl.multiple_of(home * block + c, 128), 128)] = centre
            return carry

        lax.fori_loop(0, (GROUP // 8) * (PART // 128), cell_step, 0)
        for d in range(1, groups):
            own_copy(g, sub, d).start()

    for g, sub in chunks:
        tukey(g, sub, where[g])
    own = pltpu.make_async_copy(
        loc.at[:, pl.ds(pl.multiple_of(home * block, block), block)], own_out, out_sem.at[6]
    )
    own.start()
    outs.append(own)
    for g in range(3):
        for sub in range(subs):
            for d in range(1, groups):
                own_copy(g, sub, d).wait_recv()
        at = (pl.ds(pl.multiple_of(where[g], GROUP), GROUP), slice(None))
        copy = pltpu.make_async_copy(loc.at[at], loc_out.at[at], out_sem.at[3 + g])
        copy.start()
        outs.append(copy)

    for copy in near_copies + far_copies + outer_copies:
        copy.wait_send()
    for g in range(3):
        for n in range(subs * groups):
            if (n + 1) % groups:
                z_copy(g, n, where[g]).wait_send()
    for chunk in chunks:
        for d in range(1, groups):
            own_copy(*chunk, d).wait_send()
    for copy in outs:
        copy.wait()


def finish_kernel(z_ref, loc_ref, own_ref, out_ref, own_out, buf, sems):
    seasons = z_ref.shape[0]
    copies = [pltpu.make_async_copy(own_ref, own_out, sems.at[seasons])]
    copies[0].start()
    for s in range(seasons):
        buf[s] = z_ref[s] - loc_ref[...]
        copy = pltpu.make_async_copy(buf.at[s], out_ref.at[s], sems.at[s])
        copy.start()
        copies.append(copy)
    for copy in copies:
        copy.wait()


def finish(field, loc, own):
    vmem = pl.BlockSpec(memory_space=pltpu.VMEM)
    anywhere = pl.BlockSpec(memory_space=pl.ANY)
    return pl.pallas_call(
        finish_kernel,
        out_shape=(
            jax.ShapeDtypeStruct(field.shape, F32),
            jax.ShapeDtypeStruct(own.shape, F32),
        ),
        in_specs=[vmem, vmem, anywhere],
        out_specs=(anywhere,) * 2,
        scratch_shapes=[
            pltpu.VMEM(field.shape, F32),
            pltpu.SemaphoreType.DMA((field.shape[0] + 1,)),
        ],
        compiler_params=pltpu.CompilerParams(vmem_limit_bytes=16 << 20),
        name="anomalies",
    )(field, loc, own)


def on_device(yields, quality):
    seasons, rows, cols = yields.shape
    tiles, groups = lax.axis_size("tiles"), lax.axis_size("season")
    block = cols // groups
    subs = block // PART
    dma = pltpu.SemaphoreType.DMA
    anywhere = pl.BlockSpec(memory_space=pl.ANY)
    field, loc, own = pl.pallas_call(
        functools.partial(kernel, tiles, groups),
        out_shape=(
            jax.ShapeDtypeStruct((seasons, rows, cols), F32),
            jax.ShapeDtypeStruct((rows, cols), F32),
            jax.ShapeDtypeStruct((rows, block), F32),
        ),
        in_specs=[anywhere] * 2,
        out_specs=(anywhere,) * 3,
        scratch_shapes=[
            pltpu.VMEM((seasons, rows + 2 * GROUP, cols), F32),
            pltpu.VMEM((seasons, rows + 2 * GROUP, cols), F32),
            pltpu.VMEM((2, seasons - 1, 8, cols), F32),
            pltpu.VMEM((6 * GROUP * seasons, cols + 256), BF16),
            pltpu.VMEM((seasons, rows, cols), F32),
            pltpu.VMEM((groups, seasons, rows, block), F32),
            pltpu.VMEM((rows, cols), F32),
            pltpu.VMEM((6 * GROUP, 3 * WINDOW), BF16),
            pltpu.VMEM((SPAN, WIDTH), BF16),
            pltpu.VMEM((SPAN, WIDTH), BF16),
            dma((2,)),
            dma((2,)),
            dma((2,)),
            dma((2,)),
            dma((2,)),
            dma((2,)),
            dma((2,)),
            dma((3, subs * groups)),
            dma((3, subs * groups)),
            dma((3, subs)),
            dma((3, subs, groups - 1)),
            dma((3, subs, groups - 1)),
            dma((7,)),
        ],
        compiler_params=pltpu.CompilerParams(
            collective_id=0, has_side_effects=True, vmem_limit_bytes=48 << 20
        ),
        name="field_and_location",
    )(yields, quality)
    return finish(field, loc, own)


def solution(mesh):
    placed = (P("season", "tiles", None), P("season", "tiles", None))
    return jax.shard_map(
        on_device,
        mesh=mesh,
        in_specs=placed,
        out_specs=(P("season", "tiles", None), P("tiles", "season")),
        check_vma=False,
    )
```

```python
import functools

import jax
import jax.numpy as jnp
from jax import lax
from jax.experimental import pallas as pl
from jax.experimental.pallas import tpu as pltpu
from jax.sharding import PartitionSpec as P

MESH = pl.DeviceIdType.MESH
PASSES = 4
REACH = 15
F32 = jnp.float32
BF16 = jnp.bfloat16

GROUP = 16
WINDOW = GROUP + 32
WIDTH = 256
PART = 256
SPAN = WIDTH + 256
CHUNK = 512


def tap(offset):
    value = offset.astype(F32)
    return jnp.where(jnp.abs(value) <= REACH, jnp.exp(-value * value / 128.0), 0.0)


def halves(value):
    high = value.astype(BF16)
    return high, (value - high.astype(F32)).astype(BF16)


def kernel(
    tiles, groups, y_ref, q_ref, z_out, loc_out, own_out,
    yext, qext, packed, rowwise, zbuf, cells, loc, row_band, col_high, col_low,
    own_sem, near_send, near_recv, far_send, far_recv, outer_send, outer_recv,
    z_send, z_recv, z_local, loc_send, loc_recv, out_sem,
):
    tile = lax.axis_index("tiles")
    home = lax.axis_index("season")
    core = lax.rem(tile, 2)
    seasons, rows, cols = y_ref.shape
    block = cols // groups
    subs = block // PART

    near = tile + 1 - 2 * core
    far = lax.rem(tile + 2 * core - 1 + tiles, tiles)

    loads = []
    for i, (src, dst) in enumerate(((y_ref, yext), (q_ref, qext))):
        copy = pltpu.make_async_copy(src, dst.at[:, pl.ds(GROUP, rows), :], own_sem.at[i])
        copy.start()
        loads.append(copy)

    barrier = pltpu.get_barrier_semaphore()
    partners = [(near, home), (far, home)]
    partners += [(tile, lax.rem(home + d, groups)) for d in range(1, groups)]
    for partner in partners:
        pl.semaphore_signal(barrier, inc=1, device_id=partner, device_id_type=MESH)
    pl.semaphore_wait(barrier, len(partners))

    def halo(partner, src_row, dst_row, count, send, recv):
        copies = []
        for i, (src, dst) in enumerate(((y_ref, yext), (q_ref, qext))):
            copies.append(
                pltpu.make_async_remote_copy(
                    src_ref=src.at[:, pl.ds(pl.multiple_of(src_row, 8), count), :],
                    dst_ref=dst.at[:, pl.ds(pl.multiple_of(dst_row, 8), count), :],
                    send_sem=send.at[i],
                    recv_sem=recv.at[i],
                    device_id=(partner, home),
                    device_id_type=MESH,
                )
            )
        return copies

    bottom = rows - GROUP
    past = rows + GROUP
    far_copies = halo(far, (rows - 8) * core, past - (past - 8) * core, 8, far_send, far_recv)
    for copy in far_copies:
        copy.start()
    near_copies = halo(near, bottom * (1 - core), past * core, GROUP, near_send, near_recv)
    for copy in near_copies:
        copy.start()
    for copy in loads:
        copy.wait()
    line = lax.broadcasted_iota(jnp.int32, (8, cols), 0)
    last = seasons - 1
    spare = 7 * (1 - core)
    outer_row = pl.ds(pl.multiple_of(GROUP + 8 + (rows - 24) * core, 8), 8)
    outer_copies = []
    for i, ext in enumerate((yext, qext)):
        extra = ext[last, outer_row, :]
        for s in range(last):
            row = jnp.where(core == 0, extra[s : s + 1], extra[s + 1 : s + 2])
            packed[i, s] = jnp.where(line == spare, row, ext[s, outer_row, :])
        copy = pltpu.make_async_remote_copy(
            src_ref=packed.at[i],
            dst_ref=ext.at[pl.ds(0, last), pl.ds(pl.multiple_of((past + 8) * (1 - core), 8), 8), :],
            send_sem=outer_send.at[i],
            recv_sem=outer_recv.at[i],
            device_id=(far, home),
            device_id_type=MESH,
        )
        copy.start()
        outer_copies.append(copy)

    def unpack():
        where_outer = pl.ds(pl.multiple_of((past + 8) * core, 8), 8)
        for ext in (yext, qext):
            tile_last = jnp.zeros((8, cols), F32)
            for s in range(last):
                held = ext[s, where_outer, :]
                row = jnp.where(core == 0, held[0:1], held[7:8])
                tile_last = jnp.where(line == s + 1 - core, row, tile_last)
            ext[last, where_outer, :] = tile_last

    out_row = lax.broadcasted_iota(jnp.int32, (3 * GROUP, 3 * WINDOW), 0)
    in_row = lax.broadcasted_iota(jnp.int32, (3 * GROUP, 3 * WINDOW), 1)
    same = out_row // GROUP == in_row // WINDOW
    offset = lax.rem(in_row, WINDOW) - GROUP - lax.rem(out_row, GROUP)
    high, low = halves(jnp.where(same, tap(offset), 0.0))
    row_band[pl.ds(0, 3 * GROUP), :] = high
    row_band[pl.ds(3 * GROUP, 3 * GROUP), :] = low
    in_col = lax.broadcasted_iota(jnp.int32, (SPAN, WIDTH), 0)
    out_col = lax.broadcasted_iota(jnp.int32, (SPAN, WIDTH), 1)
    high, low = halves(tap(in_col - 128 - out_col))
    col_high[...] = high
    col_low[...] = low
    count = 3 * GROUP * seasons
    edge = jnp.zeros((2 * count, 128), BF16)
    rowwise[:, pl.ds(0, 128)] = edge
    rowwise[:, pl.ds(cols + 128, 128)] = edge

    def z_copy(g, n, row0, local=False):
        sub, d = n // groups, lax.rem(n + 1, groups)
        to = lax.rem(home + d, groups)
        src = zbuf.at[
            :,
            pl.ds(pl.multiple_of(row0, GROUP), GROUP),
            pl.ds(pl.multiple_of(to * block + sub * PART, PART), PART),
        ]
        dst = cells.at[
            home,
            :,
            pl.ds(pl.multiple_of(row0, GROUP), GROUP),
            pl.ds(pl.multiple_of(sub * PART, PART), PART),
        ]
        if local:
            return pltpu.make_async_copy(src, dst, z_local.at[g, sub])
        return pltpu.make_async_remote_copy(
            src_ref=src,
            dst_ref=dst,
            send_sem=z_send.at[g, n],
            recv_sem=z_recv.at[g, n],
            device_id=(tile, to),
            device_id_type=MESH,
        )

    def smooth(g, row0):
        def row_step(n, carry):
            s, c = n // (cols // CHUNK), lax.rem(n, cols // CHUNK)
            at = (s, pl.ds(pl.multiple_of(row0, GROUP), WINDOW), pl.ds(pl.multiple_of(c * CHUNK, CHUNK), CHUNK))
            value, weight = yext[at], qext[at]
            first = weight * value
            high, low = halves(jnp.concatenate([first, first * value, weight], axis=0))
            both = jnp.dot(row_band[...], high, preferred_element_type=F32)
            rest = jnp.dot(row_band[pl.ds(0, 3 * GROUP), :], low, preferred_element_type=F32)
            high, low = halves(both[: 3 * GROUP] + both[3 * GROUP :] + rest)
            for f in range(3):
                for part, base in ((high, 0), (low, count)):
                    rowwise[
                        pl.ds(pl.multiple_of(base + f * seasons * GROUP + s * GROUP, GROUP), GROUP),
                        pl.ds(pl.multiple_of(c * CHUNK + 128, 128), CHUNK),
                    ] = part[f * GROUP : (f + 1) * GROUP]
            return carry

        lax.fori_loop(0, seasons * (cols // CHUNK), row_step, 0)

        def col_step(n, carry):
            d = lax.rem(n + 1, groups)
            col0 = lax.rem(home + d, groups) * block + (n // groups) * WIDTH
            window = rowwise[:, pl.ds(pl.multiple_of(col0, WIDTH), SPAN)]
            both = jnp.dot(window, col_high[...], preferred_element_type=F32)
            rest = jnp.dot(window[:count], col_low[...], preferred_element_type=F32)
            fields = both[:count] + both[count:] + rest
            fields = fields.reshape(3, seasons, GROUP, WIDTH)
            total = 1.0 / fields[2]
            mean = fields[0] * total
            second = fields[1] * total
            here = pl.ds(pl.multiple_of(col0, WIDTH), WIDTH)
            value = yext[:, pl.ds(pl.multiple_of(row0 + GROUP, GROUP), GROUP), here]
            zbuf[:, pl.ds(pl.multiple_of(row0, GROUP), GROUP), here] = (value - mean) * lax.rsqrt(
                second - mean * mean + 0.1
            )

            return carry

        lax.fori_loop(0, block // WIDTH * groups, col_step, 0)
        copy = pltpu.make_async_copy(
            zbuf.at[:, pl.ds(pl.multiple_of(row0, GROUP), GROUP), :],
            z_out.at[:, pl.ds(pl.multiple_of(row0, GROUP), GROUP), :],
            out_sem.at[g],
        )
        copy.start()
        return copy

    def clear(dst_row):
        qext[:, pl.ds(dst_row, GROUP), :] = jnp.zeros((seasons, GROUP, cols), F32)

    where = [GROUP, bottom * (1 - core), bottom * core]
    chunks = [(g, sub) for g in range(3) for sub in range(subs)]

    def send(g, sub):
        def send_step(d, carry):
            z_copy(g, sub * groups + d - 1, where[g]).start()
            return carry

        z_copy(g, sub * groups + groups - 1, where[g], local=True).start()
        lax.fori_loop(1, groups, send_step, 0)

    outs = [smooth(0, where[0])]
    for sub in range(subs):
        send(0, sub)
    for copy in near_copies:
        copy.wait_recv()
    outs.append(smooth(1, where[1]))
    for sub in range(subs):
        send(1, sub)
    for copy in far_copies + outer_copies:
        copy.wait_recv()
    unpack()

    @pl.when(tile == 0)
    def _():
        clear(0)

    @pl.when(tile == tiles - 1)
    def _():
        clear(past)

    outs.append(smooth(2, where[2]))
    for sub in range(subs):
        send(2, sub)

    def own_copy(g, sub, d):
        here = pl.ds(pl.multiple_of(where[g], GROUP), GROUP)
        return pltpu.make_async_remote_copy(
            src_ref=loc.at[here, pl.ds(sub * PART, PART)],
            dst_ref=loc_out.at[here, pl.ds(pl.multiple_of(home * block + sub * PART, PART), PART)],
            send_sem=loc_send.at[g, sub, d - 1],
            recv_sem=loc_recv.at[g, sub, d - 1],
            device_id=(tile, lax.rem(home + d, groups)),
            device_id_type=MESH,
        )

    def tukey(g, sub, row0):
        for n in range(sub * groups, (sub + 1) * groups):
            if (n + 1) % groups:
                z_copy(g, n, row0).wait_recv()
            else:
                z_copy(g, n, row0, local=True).wait()

        def cell_step(n, carry):
            r = row0 + 8 * (n // (PART // 128))
            c = sub * PART + 128 * lax.rem(n, PART // 128)
            field = cells[:, :, pl.ds(pl.multiple_of(r, 8), 8), pl.ds(pl.multiple_of(c, 128), 128)]
            field = field.reshape(groups * seasons, 8, 128)
            number = groups * seasons
            centre = jnp.sum(field, axis=0) / number
            for _ in range(PASSES):
                resid = field - centre
                square = resid * resid
                spread = 2.25 * (jnp.sum(square, axis=0) / number + 1.0)
                root = jnp.maximum(1.0 - square * (1.0 / spread), 0.0)
                weight = root * root
                centre = centre + jnp.sum(weight * resid, axis=0) / (jnp.sum(weight, axis=0) + 1.0)
            loc[pl.ds(pl.multiple_of(r, 8), 8), pl.ds(pl.multiple_of(c, 128), 128)] = centre
            return carry

        lax.fori_loop(0, (GROUP // 8) * (PART // 128), cell_step, 0)
        for d in range(1, groups):
            own_copy(g, sub, d).start()

    for g, sub in chunks:
        tukey(g, sub, where[g])
    mine = loc_out.at[:, pl.ds(pl.multiple_of(home * block, block), block)]
    for i, target in enumerate((own_out, mine)):
        copy = pltpu.make_async_copy(loc, target, out_sem.at[3 + i])
        copy.start()
        outs.append(copy)
    for g in range(3):
        for sub in range(subs):
            for d in range(1, groups):
                own_copy(g, sub, d).wait_recv()

    for copy in near_copies + far_copies + outer_copies:
        copy.wait_send()
    for g in range(3):
        for n in range(subs * groups):
            if (n + 1) % groups:
                z_copy(g, n, where[g]).wait_send()
    for chunk in chunks:
        for d in range(1, groups):
            own_copy(*chunk, d).wait_send()
    for copy in outs:
        copy.wait()


def finish_kernel(z_ref, loc_ref, own_ref, out_ref, own_out, buf, sems):
    seasons = z_ref.shape[0]
    copies = [pltpu.make_async_copy(own_ref, own_out, sems.at[seasons])]
    copies[0].start()
    for s in range(seasons):
        buf[s] = z_ref[s] - loc_ref[...]
        copy = pltpu.make_async_copy(buf.at[s], out_ref.at[s], sems.at[s])
        copy.start()
        copies.append(copy)
    for copy in copies:
        copy.wait()


def finish(field, loc, own):
    vmem = pl.BlockSpec(memory_space=pltpu.VMEM)
    anywhere = pl.BlockSpec(memory_space=pl.ANY)
    return pl.pallas_call(
        finish_kernel,
        out_shape=(
            jax.ShapeDtypeStruct(field.shape, F32),
            jax.ShapeDtypeStruct(own.shape, F32),
        ),
        in_specs=[vmem, vmem, anywhere],
        out_specs=(anywhere,) * 2,
        scratch_shapes=[
            pltpu.VMEM(field.shape, F32),
            pltpu.SemaphoreType.DMA((field.shape[0] + 1,)),
        ],
        compiler_params=pltpu.CompilerParams(vmem_limit_bytes=16 << 20),
        name="anomalies",
    )(field, loc, own)


def on_device(yields, quality):
    seasons, rows, cols = yields.shape
    tiles, groups = lax.axis_size("tiles"), lax.axis_size("season")
    block = cols // groups
    subs = block // PART
    dma = pltpu.SemaphoreType.DMA
    anywhere = pl.BlockSpec(memory_space=pl.ANY)
    field, loc, own = pl.pallas_call(
        functools.partial(kernel, tiles, groups),
        out_shape=(
            jax.ShapeDtypeStruct((seasons, rows, cols), F32),
            jax.ShapeDtypeStruct((rows, cols), F32),
            jax.ShapeDtypeStruct((rows, block), F32),
        ),
        in_specs=[anywhere] * 2,
        out_specs=(anywhere,) * 3,
        scratch_shapes=[
            pltpu.VMEM((seasons, rows + 2 * GROUP, cols), F32),
            pltpu.VMEM((seasons, rows + 2 * GROUP, cols), F32),
            pltpu.VMEM((2, seasons - 1, 8, cols), F32),
            pltpu.VMEM((6 * GROUP * seasons, cols + 256), BF16),
            pltpu.VMEM((seasons, rows, cols), F32),
            pltpu.VMEM((groups, seasons, rows, block), F32),
            pltpu.VMEM((rows, block), F32),
            pltpu.VMEM((6 * GROUP, 3 * WINDOW), BF16),
            pltpu.VMEM((SPAN, WIDTH), BF16),
            pltpu.VMEM((SPAN, WIDTH), BF16),
            dma((2,)),
            dma((2,)),
            dma((2,)),
            dma((2,)),
            dma((2,)),
            dma((2,)),
            dma((2,)),
            dma((3, subs * groups)),
            dma((3, subs * groups)),
            dma((3, subs)),
            dma((3, subs, groups - 1)),
            dma((3, subs, groups - 1)),
            dma((5,)),
        ],
        compiler_params=pltpu.CompilerParams(
            collective_id=0, has_side_effects=True, vmem_limit_bytes=48 << 20
        ),
        name="field_and_location",
    )(yields, quality)
    return finish(field, loc, own)


def solution(mesh):
    placed = (P("season", "tiles", None), P("season", "tiles", None))
    return jax.shard_map(
        on_device,
        mesh=mesh,
        in_specs=placed,
        out_specs=(P("season", "tiles", None), P("tiles", "season")),
        check_vma=False,
    )
```
